32 devices in a mesh: block: 16 (over z, x, core), geo: 2 (over y).
Axes of the slice: x: 2, y: 2, z: 4, core: 2. Of those that a mesh axis runs over, the one named last changes fastest.
Arguments:
- admin_vectors: bfloat16 [131072, 256], P(('block', 'geo')), may hold values from -6 to 6
- admin_bucket: int32 [131072], P(('block', 'geo')), may hold values from 0 to 15
- admin_person_class: int32 [131072], P(('block', 'geo')), may hold values from 0 to 3
- admin_holder_bucket: int32 [131072, 1], P(('block', 'geo')), may hold values from 0 to 15; in each aligned block of 4096 rows (0 to 4095, 4096 to 8191, ...) at most 384 rows name the same one
- population_vectors: bfloat16 [16384, 256], P(('block', 'geo')), may hold values from -6 to 6
- population_bucket: int32 [16384], P(('block', 'geo')), may hold values from 0 to 15
- population_person_class: int32 [16384], P(('block', 'geo')), may hold values from 0 to 3
- model_coefficients: bfloat16 [256, 1024], replicated, may hold values from -0.375 to 0.375
Outputs:
- link_out: float32 [131072], P(('block', 'geo'))
- grad: float32 [256, 1024], P('block', 'geo')
The draws below stay inside these ranges and needn't reach their ends.
Inputs may be any that keep to these rules, and one draw needn't show every extreme that they name: `admin_holder_bucket`: among the records of one device, no block index is named by more than 384 records.
All inputs are finite; a program needn't handle non-finite values.
Results may differ from the reference program's by a relative error of at most 0.00041.
Values may be sent and summed in bfloat16 or wider, within the bound.
A program may use at most 128 MiB of HBM per device.

```python
import math
import jax
import jax.numpy as jnp
import numpy as np
from jax import lax

COMPARE_WIDTH = 256
MODEL_WIDTH = 1024
REC_DEV = 4096
POPULATION_SHARE = 512
BUCKET_AMOUNT = 16
PERSON_CLASSES = 4
CAP = 384
RECORDS = 131072
POPULATION_SIZE = 16384
N_BLOCK = 16
N_GEO = 2


def place_ends(drawn, stream_key, smallest, top_value):
    index_at = [jax.random.randint(jax.random.fold_in(stream_key, axis), (), 0, length) for axis, length in enumerate(drawn.shape)]
    main_axis = drawn.shape.index(max(drawn.shape))
    neighbour = index_at[:main_axis] + [(index_at[main_axis] + 1) % drawn.shape[main_axis]] + index_at[main_axis + 1:]
    return drawn.at[tuple(index_at)].set(smallest).at[tuple(neighbour)].set(top_value)


def block_scale(stream_key, shape, pieces, low, high):
    gain = 1.0
    for position, shards_of in pieces:
        draws = jax.random.uniform(jax.random.fold_in(jax.random.fold_in(stream_key, 6), position), (shards_of,), jnp.float32, low / len(pieces), high / len(pieces))
        gain = gain * jnp.repeat(jnp.exp(draws), shape[position] // shards_of).reshape((-1,) + (1,) * (len(shape) - 1 - position))
    return gain


def rank_table(number_of, lean):
    weights = [(1 << 20) // math.isqrt(grade ** lean) + 1 for grade in range(1, number_of + 1)]
    deviation = 1 + sum(weights) // (1 << 30)
    return np.cumsum(np.array([max(1, weight // deviation) for weight in weights]))


def skewed_ids(key, dims, amount, skew):
    table = rank_table(amount, skew)
    ticket = jax.random.randint(jax.random.fold_in(key, 1), dims, 0, int(table[amount - 1]))
    standing = jnp.searchsorted(jnp.asarray(table, jnp.int32), ticket, side="right")
    return jax.random.permutation(jax.random.fold_in(key, 2), amount)[standing].astype(jnp.int32)


def assign_block(stream_key, own, number, rows, number_of, top, reach, slope):
    order = jax.random.permutation(stream_key, number_of)
    packed, common = load_shares(number_of, rows * top, reach, slope, True), load_shares(number_of, rows * top, reach, slope, False)
    places = jnp.arange(number_of)

    def named(tallies, offset_by):
        used = int((tallies > 0).sum())
        fixed = max(1, used // 4)
        passed = fixed + (places - fixed + offset_by * (used - fixed)) % max(1, number_of - fixed)
        return jnp.zeros((number_of,), jnp.int32).at[order[jnp.where(places < fixed, places, passed)]].set(jnp.asarray(tallies, jnp.int32))

    tallies = jnp.where(number % 4 == 0, named(packed, number // 4), named(common, number - number // 4 - 1))
    mixed = jax.random.permutation(jax.random.fold_in(own, 3), number_of)
    giver, receiver = mixed[0:number_of // 2 * 2:2], mixed[1:number_of // 2 * 2:2]
    slack = jnp.minimum(tallies[giver] - 1, reach - tallies[receiver]) // 2
    slack = jnp.where((giver == order[0]) | (receiver == order[0]) | (tallies[receiver] == 0), 0, jnp.maximum(slack, 0))
    passed = jax.random.randint(jax.random.fold_in(own, 4), (number_of // 2,), 0, 1 << 20) % (slack + 1)
    tallies = tallies.at[giver].add(-passed).at[receiver].add(passed)
    items = jnp.searchsorted(jnp.cumsum(tallies), jnp.arange(rows * top), side="right").astype(jnp.int32)
    listing = items.reshape(top, rows).T
    listing = listing[jax.random.permutation(jax.random.fold_in(own, 1), rows)]
    offset_by = jax.random.randint(jax.random.fold_in(own, 2), (rows, 1), 0, top)
    return jnp.take_along_axis(listing, (jnp.arange(top)[None, :] + offset_by) % top, axis=1)


def load_shares(count, total, most, lean, full):
    loads = [(1 << 20) // math.isqrt(rank ** lean) + 1 for rank in range(1, count + 1)]
    largest = most if full else min(most, max(-(-total // count), total * loads[0] // sum(loads)))
    least = 1 if total - largest >= count - 1 else 0
    holding, rest = [largest] + [least] * (count - 1), total - largest - least * (count - 1)
    while rest > 0:
        free = [i for i in range(1, count) if holding[i] < largest] or [i for i in range(1, count) if holding[i] < most]
        pool, budget = sum([loads[i] for i in free]), rest
        for i in free:
            addition = min(most - holding[i], max(1, budget * loads[i] // pool), rest)
            holding[i] = holding[i] + addition
            rest = rest - addition
    return np.array(holding)


def bell_draw(stream_key, extent, scale, reach, shards=(), kind=jnp.bfloat16):
    array = scale * jax.random.normal(stream_key, extent, jnp.float32)
    if shards:
        array = array * block_scale(stream_key, extent, shards, -0.22, 0.18)
    return jnp.clip(array, -reach, reach).astype(kind)


def setup_inputs(seed: int = 0) -> dict:
    key_of = jax.random.split(jax.random.key(seed), 9)
    admin_vectors = bell_draw(key_of[0], (RECORDS, COMPARE_WIDTH), 1.0, 6.0, ((0, 32),))
    admin_bucket = place_ends(skewed_ids(key_of[1], (RECORDS,), BUCKET_AMOUNT, 2), jax.random.fold_in(key_of[1], 3), 0, BUCKET_AMOUNT - 1).astype(jnp.int32)
    admin_person_class = place_ends(jax.random.randint(key_of[2], (RECORDS,), 0, PERSON_CLASSES), jax.random.fold_in(key_of[2], 1), 0, PERSON_CLASSES - 1).astype(jnp.int32)
    admin_holder_bucket_keys = jax.random.split(jax.random.fold_in(key_of[3], 1), RECORDS // REC_DEV)
    admin_holder_bucket_turns = jax.random.permutation(jax.random.fold_in(key_of[3], 3), RECORDS // REC_DEV)
    admin_holder_bucket = jax.vmap(lambda own, number: assign_block(jax.random.fold_in(key_of[3], 2), own, number, REC_DEV, N_BLOCK, 1, CAP, 2))(admin_holder_bucket_keys, admin_holder_bucket_turns).reshape((RECORDS, 1))
    population_vectors = bell_draw(key_of[4], (POPULATION_SIZE, COMPARE_WIDTH), 1.0, 6.0, ((0, 32),))
    population_bucket = place_ends(jax.random.randint(key_of[5], (POPULATION_SIZE,), 0, BUCKET_AMOUNT), jax.random.fold_in(key_of[5], 1), 0, BUCKET_AMOUNT - 1).astype(jnp.int32)
    population_person_class = place_ends(jax.random.randint(key_of[6], (POPULATION_SIZE,), 0, PERSON_CLASSES), jax.random.fold_in(key_of[6], 1), 0, PERSON_CLASSES - 1).astype(jnp.int32)
    model_coefficients = bell_draw(key_of[7], (COMPARE_WIDTH, MODEL_WIDTH), COMPARE_WIDTH ** -0.5, 0.375)
    return {"admin_vectors": admin_vectors, "admin_bucket": admin_bucket, "admin_person_class": admin_person_class, "admin_holder_bucket": admin_holder_bucket, "population_vectors": population_vectors, "population_bucket": population_bucket, "population_person_class": population_person_class, "model_coefficients": model_coefficients}


def ranks(dest):
    onehot = (dest[:, None] == jnp.arange(N_BLOCK, dtype=jnp.int32)[None, :]).astype(jnp.int32)
    return jnp.sum((jnp.cumsum(onehot, axis=0) - 1) * onehot, axis=1).astype(jnp.int32)


def reference(admin_vectors, admin_bucket, admin_person_class, admin_holder_bucket, population_vectors, population_bucket, population_person_class, model_coefficients):
    group_size = N_BLOCK * N_GEO
    dest = admin_holder_bucket[:, 0].astype(jnp.int32)
    order = jax.vmap(ranks)(dest.reshape(group_size, REC_DEV)).reshape(-1)
    device = (jnp.arange(RECORDS, dtype=jnp.int32) // REC_DEV).astype(jnp.int32)
    owner = (dest * N_GEO + device % N_GEO).astype(jnp.int32)
    slot = ((device // N_GEO) * CAP + order).astype(jnp.int32)
    lookup_matrix = jnp.full((group_size, N_BLOCK * CAP), -1, jnp.int32).at[owner, slot].set(jnp.arange(RECORDS, dtype=jnp.int32))
    proj_all = jnp.dot(admin_vectors, model_coefficients, preferred_element_type=jnp.float32).astype(jnp.bfloat16)
    population_entries = population_vectors.reshape(group_size, POPULATION_SHARE, COMPARE_WIDTH)
    population_buckets = population_bucket.reshape(group_size, POPULATION_SHARE)
    population_persons = population_person_class.reshape(group_size, POPULATION_SHARE)
    normalizer = 1.0 / (MODEL_WIDTH ** 0.5)

    def iteration(accumulated, inputs):
        idx, population_entry, ckey, cent = inputs
        valid = idx >= 0
        safe = jnp.maximum(idx, 0).astype(jnp.int32)
        mapped_entry = jnp.where(valid[:, None], proj_all[safe], jnp.zeros((), jnp.bfloat16))
        xrow = jnp.where(valid[:, None], admin_vectors[safe], jnp.zeros((), jnp.bfloat16))
        rkey = jnp.where(valid, admin_bucket[safe], -1)
        rent = admin_person_class[safe]
        population_mapped = jnp.dot(population_entry, model_coefficients, preferred_element_type=jnp.float32).astype(jnp.bfloat16)
        similarity = jnp.dot(mapped_entry, population_mapped.T, preferred_element_type=jnp.float32) * normalizer
        possible_couples = rkey[:, None] == ckey[None, :]
        match_labels = (possible_couples & (rent[:, None] == cent[None, :])).astype(jnp.float32)
        prob = jax.nn.sigmoid(similarity)
        link = jnp.sum(jnp.where(possible_couples, prob, 0.0), axis=1)
        residual_error = jnp.where(possible_couples, prob - match_labels, 0.0).astype(jnp.bfloat16)
        admin_mapped_slope = (jnp.dot(residual_error, population_mapped, preferred_element_type=jnp.float32) * normalizer).astype(jnp.bfloat16)
        population_mapped_slope = (lax.dot_general(residual_error, mapped_entry, (((0,), (0,)), ((), ())), preferred_element_type=jnp.float32) * normalizer).astype(jnp.bfloat16)
        summand = lax.dot_general(xrow, admin_mapped_slope, (((0,), (0,)), ((), ())), preferred_element_type=jnp.float32)
        summand = summand + lax.dot_general(population_entry, population_mapped_slope, (((0,), (0,)), ((), ())), preferred_element_type=jnp.float32)
        return accumulated + summand, link

    accumulated, joined_couples = lax.scan(iteration, jnp.zeros((COMPARE_WIDTH, MODEL_WIDTH), jnp.float32), (lookup_matrix, population_entries, population_buckets, population_persons))
    link_out = joined_couples[owner, slot]
    grad = accumulated * (1.0 / (RECORDS ** 0.5))
    return link_out, grad
```

```python
import functools

import jax
import jax.numpy as jnp
from jax import lax
from jax.experimental import pallas as pl
from jax.experimental.pallas import tpu as pltpu
from jax.sharding import PartitionSpec as P

F32 = jnp.float32
BF16 = jnp.bfloat16
LANES = 512


def over_rows(left, right):
    return lax.dot_general(left, right, (((0,), (0,)), ((), ())), preferred_element_type=F32)


def over_columns(left, right):
    return lax.dot_general(left, right, (((1,), (1,)), ((), ())), preferred_element_type=F32)


def plain(left, right):
    return jnp.dot(left, right, preferred_element_type=F32)


def order_kernel(groups, cap, dest_ref, code_ref, x_ref, m_ref, proj_ref, rows_ref, slots_ref, rank_ref):
    owner = pl.program_id(0)
    count = dest_ref.shape[1]

    @pl.when(owner == 0)
    def _():
        width = 256
        before = lax.broadcasted_iota(jnp.int32, (width, width), 0)
        after = lax.broadcasted_iota(jnp.int32, (width, width), 1)
        upper = jnp.where(before <= after, 1.0, 0.0).astype(BF16)
        carry = jnp.zeros((groups, 1), F32)
        slots = jnp.zeros((groups, cap), F32)
        for at in range(0, count, width):
            span = pl.ds(at, width)
            owners = lax.broadcasted_iota(jnp.int32, (groups, width), 0)
            onehot = jnp.where(owners == dest_ref[:, span], 1.0, 0.0)
            running = plain(onehot.astype(BF16), upper) + carry
            rank = (jnp.sum(running * onehot, axis=0, keepdims=True) - 1.0).astype(jnp.int32)
            rank_ref[:, span] = rank
            carry = running[:, width - 1 : width]
            places = lax.broadcasted_iota(jnp.int32, (cap, width), 0)
            placed = jnp.where(places == rank, 1.0, 0.0).astype(BF16)
            slots = slots + over_columns((onehot * code_ref[:, span]).astype(BF16), placed)
        slots_ref[...] = slots

    rows = jnp.zeros((cap, x_ref.shape[1]), F32)
    places = lax.broadcasted_iota(jnp.int32, (cap, LANES), 0)
    for at in range(0, count, LANES):
        span = pl.ds(at, LANES)
        mine = jnp.where(dest_ref[:, span] == owner, rank_ref[:, span], -1)
        placed = jnp.where(places == mine, 1.0, 0.0).astype(BF16)
        rows = rows + plain(placed, x_ref[span, :])
    rows = rows.astype(BF16)
    rows_ref[0] = rows
    proj_ref[0] = plain(rows, m_ref[...]).astype(BF16)


def score_kernel(
    groups, cap, grad_scale,
    dest_ref, rank_ref, slots_ref, m_ref, proj_ref, rows_ref, census_ref,
    link_ref, sym_ref, total_ref, sums_ref,
):
    owner = pl.program_id(0)
    count = dest_ref.shape[1]
    feat = rows_ref.shape[2]
    hidden = m_ref.shape[1]
    people = census_ref.shape[1] // 16 * 16 - 16

    census = census_ref[0, :people, :]
    labels = census_ref[0, people:, :].astype(F32)
    columns = []
    for part in range(people // feat):
        row = jnp.broadcast_to(labels[part : part + 1, :], (128, feat))
        columns.append(jnp.transpose(row)[:, :1])
    label = jnp.concatenate(columns, axis=0)
    key = jnp.floor((label - 1.0) * 0.25)
    slot_label = slots_ref[pl.ds(owner, 1), :]
    slot_key = jnp.floor((slot_label - 1.0) * 0.25)

    mapped = plain(census, m_ref[...]).astype(BF16)
    raw = over_columns(mapped, proj_ref[0])
    prob = 0.5 * jnp.tanh(raw * (0.5 / hidden**0.5)) + 0.5
    prob = jnp.where(key == slot_key, prob, 0.0)
    sums_ref[pl.ds(owner, 1), :] = jnp.sum(prob, axis=0, keepdims=True)
    resid = (prob - jnp.where(label == slot_label, 1.0, 0.0)).astype(BF16)
    pulled = plain(resid, rows_ref[0])
    high = pulled.astype(BF16)
    low = (pulled - high.astype(F32)).astype(BF16)
    step = over_rows(census, high) + over_rows(census, low)

    @pl.when(owner == 0)
    def _():
        total_ref[...] = step

    @pl.when(owner > 0)
    def _():
        total_ref[...] += step

    @pl.when(owner == groups - 1)
    def _():
        total = total_ref[...]
        sym_ref[...] = (total + jnp.transpose(total)) * grad_scale
        sums = sums_ref[...]
        top = sums.astype(BF16)
        rest = (sums - top.astype(F32)).astype(BF16)
        places = lax.broadcasted_iota(jnp.int32, (cap, LANES), 0)
        owners = lax.broadcasted_iota(jnp.int32, (groups, LANES), 0)
        for at in range(0, count, LANES):
            span = pl.ds(at, LANES)
            onehot = jnp.where(owners == dest_ref[:, span], 1.0, 0.0).astype(BF16)
            spread = over_rows(top, onehot) + over_rows(rest, onehot)
            spread = jnp.where(places == rank_ref[:, span], spread, 0.0)
            link_ref[:, span] = jnp.sum(spread, axis=0, keepdims=True)


def body(
    admin_vectors,
    admin_bucket,
    admin_person_class,
    admin_holder_bucket,
    population_vectors,
    population_bucket,
    population_person_class,
    model_coefficients,
):
    count, feat = admin_vectors.shape
    groups = lax.axis_size("block")
    regions = lax.axis_size("geo")
    cap = 3 * count // (2 * groups)
    hidden = model_coefficients.shape[1]
    people = population_vectors.shape[0]
    dest = admin_holder_bucket.reshape(1, count)
    code = (admin_bucket * 4 + admin_person_class + 1).astype(F32).reshape(1, count)
    census_code = (population_bucket * 4 + population_person_class + 1).astype(BF16)
    census_code = census_code.reshape(people // feat, feat)
    census_code = jnp.pad(census_code, ((0, 16 - people // feat), (0, 0)))
    census = lax.all_gather(jnp.concatenate([population_vectors, census_code], axis=0), "block")
    tall = people + 16

    def whole(shape):
        return pl.BlockSpec(shape, lambda o: (0,) * len(shape))

    def each(shape):
        return pl.BlockSpec((1,) + shape, lambda o: (o, 0, 0))

    proj, rows, slots, rank = pl.pallas_call(
        functools.partial(order_kernel, groups, cap),
        grid=(groups,),
        in_specs=[whole((1, count)), whole((1, count)), whole((count, feat)), whole((feat, hidden))],
        out_specs=[each((cap, hidden)), each((cap, feat)), whole((groups, cap)), whole((1, count))],
        out_shape=[
            jax.ShapeDtypeStruct((groups, cap, hidden), BF16),
            jax.ShapeDtypeStruct((groups, cap, feat), BF16),
            jax.ShapeDtypeStruct((groups, cap), F32),
            jax.ShapeDtypeStruct((1, count), jnp.int32),
        ],
        compiler_params=pltpu.CompilerParams(vmem_limit_bytes=40 << 20),
        cost_estimate=pl.CostEstimate(
            flops=2 * groups * cap * feat * (count + hidden), bytes_accessed=20 << 20, transcendentals=0
        ),
        name="order_records",
    )(dest, code, admin_vectors, model_coefficients)

    grad_scale = 1.0 / hidden**0.5 / (count * groups * regions) ** 0.5
    link, sym = pl.pallas_call(
        functools.partial(score_kernel, groups, cap, grad_scale),
        grid=(groups,),
        in_specs=[
            whole((1, count)),
            whole((1, count)),
            whole((groups, cap)),
            whole((feat, hidden)),
            each((cap, hidden)),
            each((cap, feat)),
            each((tall, feat)),
        ],
        out_specs=[whole((1, count)), whole((feat, feat))],
        out_shape=[jax.ShapeDtypeStruct((1, count), F32), jax.ShapeDtypeStruct((feat, feat), F32)],
        scratch_shapes=[pltpu.VMEM((feat, feat), F32), pltpu.VMEM((groups, cap), F32)],
        compiler_params=pltpu.CompilerParams(vmem_limit_bytes=40 << 20),
        cost_estimate=pl.CostEstimate(
            flops=2 * groups * people * (feat * hidden + cap * hidden + cap * feat + 2 * feat * feat),
            bytes_accessed=20 << 20,
            transcendentals=groups * people * cap,
        ),
        name="score_pairs",
    )(dest, rank, slots, model_coefficients, proj, rows, census)

    sym = lax.psum(sym, ("block", "geo"))
    rows_each = feat // groups
    cols_each = hidden // regions
    mine = lax.dynamic_slice(sym, (lax.axis_index("block") * rows_each, 0), (rows_each, feat))
    model = lax.dynamic_slice(
        model_coefficients, (0, lax.axis_index("geo") * cols_each), (feat, cols_each)
    )
    grad = jnp.dot(mine, model.astype(F32), precision=lax.Precision.HIGHEST)
    return (link.reshape(count), grad)


def solution(mesh):
    placed = (
        P(("block", "geo"), None),
        P(("block", "geo")),
        P(("block", "geo")),
        P(("block", "geo"), None),
        P(("block", "geo"), None),
        P(("block", "geo")),
        P(("block", "geo")),
        P(),
    )
    return jax.shard_map(
        body,
        mesh=mesh,
        in_specs=placed,
        out_specs=(P(("block", "geo")), P("block", "geo")),
        check_vma=False,
    )
```

```python
import functools

import jax
import jax.numpy as jnp
from jax import lax
from jax.experimental import pallas as pl
from jax.experimental.pallas import tpu as pltpu
from jax.sharding import PartitionSpec as P

F32 = jnp.float32
BF16 = jnp.bfloat16
LANES = 512
MESH = pl.DeviceIdType.MESH


def over_rows(left, right):
    return lax.dot_general(left, right, (((0,), (0,)), ((), ())), preferred_element_type=F32)


def over_columns(left, right):
    return lax.dot_general(left, right, (((1,), (1,)), ((), ())), preferred_element_type=F32)


def plain(left, right):
    return jnp.dot(left, right, preferred_element_type=F32)


def gather_plan(groups, own_ref, all_ref, send1, recv1, send2, recv2, send3, recv3):
    outer, inner = 4, groups // 8
    block = lax.axis_index("block")
    core = lax.rem(block, 2)
    x = lax.rem(block // 2, inner)
    z = block // (2 * inner)

    def number(z, x, core):
        return (z * inner + x) * 2 + core

    def held(k, j):
        if k == 0 and j == 0:
            return own_ref
        return all_ref.at[number(lax.rem(z + outer - k, outer), lax.rem(x + inner - j, inner), core)]

    def slot(k, j):
        return all_ref.at[number(lax.rem(z + outer - k, outer), lax.rem(x + inner - j, inner), core)]

    def copy(source, target, send, recv, peer):
        return pltpu.make_async_remote_copy(
            src_ref=source, dst_ref=target, send_sem=send, recv_sem=recv,
            device_id={"block": peer}, device_id_type=MESH,
        )

    peers = [number(lax.rem(z + k, outer), x, core) for k in range(1, outer)]
    peers += [number(z, lax.rem(x + j, inner), core) for j in range(1, inner)]
    peers += [number(z, x, 1 - core)]

    def along_outer(k):
        return copy(own_ref, slot(0, 0), send1.at[k], recv1.at[k], peers[k - 1])

    def along_inner(k, j):
        at = k * inner + j
        return copy(held(k, 0), slot(k, 0), send2.at[at], recv2.at[at], number(z, lax.rem(x + j, inner), core))

    def to_core(k, j):
        at = k * inner + j
        return copy(held(k, j), slot(k, j), send3.at[at], recv3.at[at], peers[-1])

    return outer, inner, block, peers, along_outer, along_inner, to_core


def gather_step(groups, step, own_ref, all_ref, local, *sems):
    outer, inner, block, peers, along_outer, along_inner, to_core = gather_plan(
        groups, own_ref, all_ref, *sems
    )

    @pl.when(step == 0)
    def _():
        barrier = pltpu.get_barrier_semaphore()
        for peer in peers:
            pl.semaphore_signal(barrier, inc=1, device_id={"block": peer}, device_id_type=MESH)
        pl.semaphore_wait(barrier, len(peers))
        for k in (2, 3, 1):
            along_outer(k).start()
        for j in range(1, inner):
            along_inner(0, j).start()
        to_core(0, 0).start()
        pltpu.make_async_copy(own_ref, all_ref.at[block], local).start()

    for k in range(1, outer):

        @pl.when(step == (2, 6, 8, 10)[k])
        def _(k=k):
            along_outer(k).wait_recv()
            for j in range(1, inner):
                along_inner(k, j).start()
            to_core(k, 0).start()

    for k in range(outer):

        @pl.when(step == (7, 10, 12, 14)[k])
        def _(k=k):
            for j in range(1, inner):
                along_inner(k, j).wait_recv()
                to_core(k, j).start()

    @pl.when(step == groups - 1)
    def _():
        pltpu.make_async_copy(own_ref, all_ref.at[block], local).wait()
        for k in range(1, outer):
            along_outer(k).wait_send()
        for k in range(outer):
            for j in range(1, inner):
                along_inner(k, j).wait_send()
            for j in range(inner):
                to_core(k, j).wait()


def order_kernel(
    groups, cap, dest_ref, code_ref, x_ref, m_ref, own_ref, proj_ref, rows_ref, slots_ref, rank_ref, all_ref,
    local, *sems,
):
    owner = pl.program_id(0)
    count = dest_ref.shape[1]
    gather_step(groups, owner, own_ref, all_ref, local, *sems)

    @pl.when(owner == 0)
    def _():
        width = 256
        before = lax.broadcasted_iota(jnp.int32, (width, width), 0)
        after = lax.broadcasted_iota(jnp.int32, (width, width), 1)
        upper = jnp.where(before <= after, 1.0, 0.0).astype(BF16)
        carry = jnp.zeros((groups, 1), F32)
        slots = jnp.zeros((groups, cap), F32)
        for at in range(0, count, width):
            span = pl.ds(at, width)
            owners = lax.broadcasted_iota(jnp.int32, (groups, width), 0)
            onehot = jnp.where(owners == dest_ref[:, span], 1.0, 0.0)
            running = plain(onehot.astype(BF16), upper) + carry
            rank = (jnp.sum(running * onehot, axis=0, keepdims=True) - 1.0).astype(jnp.int32)
            rank_ref[:, span] = rank
            carry = running[:, width - 1 : width]
            places = lax.broadcasted_iota(jnp.int32, (cap, width), 0)
            placed = jnp.where(places == rank, 1.0, 0.0).astype(BF16)
            slots = slots + over_columns((onehot * code_ref[:, span]).astype(BF16), placed)
        slots_ref[...] = slots

    rows = jnp.zeros((cap, x_ref.shape[1]), F32)
    places = lax.broadcasted_iota(jnp.int32, (cap, LANES), 0)
    for at in range(0, count, LANES):
        span = pl.ds(at, LANES)
        mine = jnp.where(dest_ref[:, span] == owner, rank_ref[:, span], -1)
        placed = jnp.where(places == mine, 1.0, 0.0).astype(BF16)
        rows = rows + plain(placed, x_ref[span, :])
    rows = rows.astype(BF16)
    rows_ref[0] = rows
    proj_ref[0] = plain(rows, m_ref[...]).astype(BF16)


def score_kernel(
    groups, cap, grad_scale,
    dest_ref, rank_ref, slots_ref, m_ref, proj_ref, rows_ref, census_ref,
    link_ref, sym_ref, total_ref, sums_ref,
):
    owner = pl.program_id(0)
    count = dest_ref.shape[1]
    feat = rows_ref.shape[2]
    hidden = m_ref.shape[1]
    people = census_ref.shape[1] // 16 * 16 - 16

    census = census_ref[0, :people, :]
    labels = census_ref[0, people:, :].astype(F32)
    columns = []
    for part in range(people // feat):
        row = jnp.broadcast_to(labels[part : part + 1, :], (128, feat))
        columns.append(jnp.transpose(row)[:, :1])
    label = jnp.concatenate(columns, axis=0)
    key = jnp.floor((label - 1.0) * 0.25)
    slot_label = slots_ref[pl.ds(owner, 1), :]
    slot_key = jnp.floor((slot_label - 1.0) * 0.25)

    mapped = plain(census, m_ref[...]).astype(BF16)
    raw = over_columns(mapped, proj_ref[0])
    prob = 0.5 * jnp.tanh(raw * (0.5 / hidden**0.5)) + 0.5
    prob = jnp.where(key == slot_key, prob, 0.0)
    sums_ref[pl.ds(owner, 1), :] = jnp.sum(prob, axis=0, keepdims=True)
    resid = (prob - jnp.where(label == slot_label, 1.0, 0.0)).astype(BF16)
    pulled = plain(resid, rows_ref[0])
    high = pulled.astype(BF16)
    low = (pulled - high.astype(F32)).astype(BF16)
    step = over_rows(census, high) + over_rows(census, low)

    @pl.when(owner == 0)
    def _():
        total_ref[...] = step

    @pl.when(owner > 0)
    def _():
        total_ref[...] += step

    @pl.when(owner == groups - 1)
    def _():
        total = total_ref[...]
        sym_ref[...] = (total + jnp.transpose(total)) * grad_scale
        sums = sums_ref[...]
        top = sums.astype(BF16)
        rest = (sums - top.astype(F32)).astype(BF16)
        places = lax.broadcasted_iota(jnp.int32, (cap, LANES), 0)
        owners = lax.broadcasted_iota(jnp.int32, (groups, LANES), 0)
        for at in range(0, count, LANES):
            span = pl.ds(at, LANES)
            onehot = jnp.where(owners == dest_ref[:, span], 1.0, 0.0).astype(BF16)
            spread = over_rows(top, onehot) + over_rows(rest, onehot)
            spread = jnp.where(places == rank_ref[:, span], spread, 0.0)
            link_ref[:, span] = jnp.sum(spread, axis=0, keepdims=True)


def reduce_kernel(groups, regions, sym_ref, m_ref, grad_ref, got, mid, send1, recv1, send2, recv2):
    block = lax.axis_index("block")
    region = lax.axis_index("geo")
    rows = got.shape[1]
    cols = grad_ref.shape[1]
    barrier = pltpu.get_barrier_semaphore()
    for k in range(1, groups):
        pl.semaphore_signal(
            barrier, inc=1, device_id={"block": lax.rem(block + k, groups)}, device_id_type=MESH
        )
    for k in range(1, regions):
        pl.semaphore_signal(
            barrier, inc=1, device_id={"geo": lax.rem(region + k, regions)}, device_id_type=MESH
        )
    pl.semaphore_wait(barrier, groups + regions - 2)

    copies = []
    for k in range(1, groups):
        peer = lax.rem(block + k, groups)
        copy = pltpu.make_async_remote_copy(
            src_ref=sym_ref.at[pl.ds(pl.multiple_of(peer * rows, rows), rows), :],
            dst_ref=got.at[k],
            send_sem=send1.at[k],
            recv_sem=recv1.at[k],
            device_id={"block": peer},
            device_id_type=MESH,
        )
        copy.start()
        copies.append(copy)
    total = sym_ref[pl.ds(pl.multiple_of(block * rows, rows), rows), :]
    for k in range(1, groups):
        copies[k - 1].wait_recv()
        total = total + got[k]
    mid[0] = total
    crossing = []
    for k in range(1, regions):
        copy = pltpu.make_async_remote_copy(
            src_ref=mid.at[0],
            dst_ref=mid.at[k],
            send_sem=send2.at[k],
            recv_sem=recv2.at[k],
            device_id={"geo": lax.rem(region + k, regions)},
            device_id_type=MESH,
        )
        copy.start()
        crossing.append(copy)
    for k in range(1, regions):
        crossing[k - 1].wait_recv()
        total = total + mid[k]
    model = m_ref[:, pl.ds(pl.multiple_of(region * cols, cols), cols)]
    first = total.astype(BF16)
    left = total - first.astype(F32)
    second = left.astype(BF16)
    third = (left - second.astype(F32)).astype(BF16)
    grad_ref[...] = plain(first, model) + plain(second, model) + plain(third, model)
    for copy in copies + crossing:
        copy.wait_send()


def body(
    admin_vectors,
    admin_bucket,
    admin_person_class,
    admin_holder_bucket,
    population_vectors,
    population_bucket,
    population_person_class,
    model_coefficients,
):
    count, feat = admin_vectors.shape
    groups = lax.axis_size("block")
    regions = lax.axis_size("geo")
    cap = 3 * count // (2 * groups)
    hidden = model_coefficients.shape[1]
    people = population_vectors.shape[0]
    dest = admin_holder_bucket.reshape(1, count)
    code = (admin_bucket * 4 + admin_person_class + 1).astype(F32).reshape(1, count)
    census_code = (population_bucket * 4 + population_person_class + 1).astype(BF16)
    census_code = census_code.reshape(people // feat, feat)
    census_code = jnp.pad(census_code, ((0, 16 - people // feat), (0, 0)))
    census = jnp.concatenate([population_vectors, census_code], axis=0)
    tall = people + 16

    def whole(shape):
        return pl.BlockSpec(shape, lambda o: (0,) * len(shape))

    def each(shape):
        return pl.BlockSpec((1,) + shape, lambda o: (o, 0, 0))

    proj, rows, slots, rank, census = pl.pallas_call(
        functools.partial(order_kernel, groups, cap),
        grid=(groups,),
        in_specs=[whole((1, count)), whole((1, count)), whole((count, feat)), whole((feat, hidden))]
        + [pl.BlockSpec(memory_space=pl.ANY)],
        out_specs=[each((cap, hidden)), each((cap, feat)), whole((groups, cap)), whole((1, count))]
        + [pl.BlockSpec(memory_space=pl.ANY)],
        out_shape=[
            jax.ShapeDtypeStruct((groups, cap, hidden), BF16),
            jax.ShapeDtypeStruct((groups, cap, feat), BF16),
            jax.ShapeDtypeStruct((groups, cap), F32),
            jax.ShapeDtypeStruct((1, count), jnp.int32),
            jax.ShapeDtypeStruct((groups, tall, feat), BF16),
        ],
        scratch_shapes=[pltpu.SemaphoreType.DMA]
        + [pltpu.SemaphoreType.DMA((4,))] * 2
        + [pltpu.SemaphoreType.DMA((groups // 2,))] * 4,
        compiler_params=pltpu.CompilerParams(
            vmem_limit_bytes=40 << 20, collective_id=1, has_side_effects=True
        ),
        cost_estimate=pl.CostEstimate(
            flops=2 * groups * cap * feat * (count + hidden), bytes_accessed=20 << 20, transcendentals=0
        ),
        name="order_records",
    )(dest, code, admin_vectors, model_coefficients, census)

    grad_scale = 1.0 / hidden**0.5 / (count * groups * regions) ** 0.5
    link, sym = pl.pallas_call(
        functools.partial(score_kernel, groups, cap, grad_scale),
        grid=(groups,),
        in_specs=[
            whole((1, count)),
            whole((1, count)),
            whole((groups, cap)),
            whole((feat, hidden)),
            each((cap, hidden)),
            each((cap, feat)),
            each((tall, feat)),
        ],
        out_specs=[whole((1, count)), whole((feat, feat))],
        out_shape=[jax.ShapeDtypeStruct((1, count), F32), jax.ShapeDtypeStruct((feat, feat), F32)],
        scratch_shapes=[pltpu.VMEM((feat, feat), F32), pltpu.VMEM((groups, cap), F32)],
        compiler_params=pltpu.CompilerParams(vmem_limit_bytes=40 << 20),
        cost_estimate=pl.CostEstimate(
            flops=2 * groups * people * (feat * hidden + cap * hidden + cap * feat + 2 * feat * feat),
            bytes_accessed=20 << 20,
            transcendentals=groups * people * cap,
        ),
        name="score_pairs",
    )(dest, rank, slots, model_coefficients, proj, rows, census)

    rows_each = feat // groups
    cols_each = hidden // regions
    grad = pl.pallas_call(
        functools.partial(reduce_kernel, groups, regions),
        in_specs=[pl.BlockSpec(memory_space=pltpu.VMEM)] * 2,
        out_specs=pl.BlockSpec(memory_space=pltpu.VMEM),
        out_shape=jax.ShapeDtypeStruct((rows_each, cols_each), F32),
        scratch_shapes=[
            pltpu.VMEM((groups, rows_each, feat), F32),
            pltpu.VMEM((regions, rows_each, feat), F32),
            pltpu.SemaphoreType.DMA((groups,)),
            pltpu.SemaphoreType.DMA((groups,)),
            pltpu.SemaphoreType.DMA((regions,)),
            pltpu.SemaphoreType.DMA((regions,)),
        ],
        compiler_params=pltpu.CompilerParams(collective_id=0, has_side_effects=True),
        cost_estimate=pl.CostEstimate(
            flops=6 * rows_each * cols_each * feat, bytes_accessed=1 << 20, transcendentals=0
        ),
        name="reduce_gradient",
    )(sym, model_coefficients)
    return (link.reshape(count), grad)


def solution(mesh):
    placed = (
        P(("block", "geo"), None),
        P(("block", "geo")),
        P(("block", "geo")),
        P(("block", "geo"), None),
        P(("block", "geo"), None),
        P(("block", "geo")),
        P(("block", "geo")),
        P(),
    )
    return jax.shard_map(
        body,
        mesh=mesh,
        in_specs=placed,
        out_specs=(P(("block", "geo")), P("block", "geo")),
        check_vma=False,
    )
```

```python
import functools

import jax
import jax.numpy as jnp
from jax import lax
from jax.experimental import pallas as pl
from jax.experimental.pallas import tpu as pltpu
from jax.sharding import PartitionSpec as P

F32 = jnp.float32
BF16 = jnp.bfloat16
LANES = 512
MESH = pl.DeviceIdType.MESH


def over_rows(left, right):
    return lax.dot_general(left, right, (((0,), (0,)), ((), ())), preferred_element_type=F32)


def over_columns(left, right):
    return lax.dot_general(left, right, (((1,), (1,)), ((), ())), preferred_element_type=F32)


def plain(left, right):
    return jnp.dot(left, right, preferred_element_type=F32)


def gather_plan(groups, own_ref, all_ref, send1, recv1, send2, recv2, send3, recv3):
    outer, inner = 4, groups // 8
    block = lax.axis_index("block")
    core = lax.rem(block, 2)
    x = lax.rem(block // 2, inner)
    z = block // (2 * inner)

    def number(z, x, core):
        return (z * inner + x) * 2 + core

    def held(k, j):
        if k == 0 and j == 0:
            return own_ref
        return all_ref.at[number(lax.rem(z + outer - k, outer), lax.rem(x + inner - j, inner), core)]

    def slot(k, j):
        return all_ref.at[number(lax.rem(z + outer - k, outer), lax.rem(x + inner - j, inner), core)]

    def copy(source, target, send, recv, peer):
        return pltpu.make_async_remote_copy(
            src_ref=source, dst_ref=target, send_sem=send, recv_sem=recv,
            device_id={"block": peer}, device_id_type=MESH,
        )

    peers = [number(lax.rem(z + k, outer), x, core) for k in range(1, outer)]
    peers += [number(z, lax.rem(x + j, inner), core) for j in range(1, inner)]
    peers += [number(z, x, 1 - core)]

    def along_outer(k):
        return copy(own_ref, slot(0, 0), send1.at[k], recv1.at[k], peers[k - 1])

    def along_inner(k, j):
        at = k * inner + j
        return copy(held(k, 0), slot(k, 0), send2.at[at], recv2.at[at], number(z, lax.rem(x + j, inner), core))

    def to_core(k, j):
        at = k * inner + j
        return copy(held(k, j), slot(k, j), send3.at[at], recv3.at[at], peers[-1])

    return outer, inner, block, peers, along_outer, along_inner, to_core


def gather_step(groups, step, own_ref, all_ref, local, *sems):
    outer, inner, block, peers, along_outer, along_inner, to_core = gather_plan(
        groups, own_ref, all_ref, *sems
    )

    @pl.when(step == 0)
    def _():
        barrier = pltpu.get_barrier_semaphore()
        for peer in peers:
            pl.semaphore_signal(barrier, inc=1, device_id={"block": peer}, device_id_type=MESH)
        pl.semaphore_wait(barrier, len(peers))
        for k in (2, 3, 1):
            along_outer(k).start()
        for j in range(1, inner):
            along_inner(0, j).start()
        to_core(0, 0).start()
        pltpu.make_async_copy(own_ref, all_ref.at[block], local).start()

    for k in range(1, outer):

        @pl.when(step == (0, 10, 11, 12)[k])
        def _(k=k):
            along_outer(k).wait_recv()
            for j in range(1, inner):
                along_inner(k, j).start()
            to_core(k, 0).start()

    for k in range(outer):

        @pl.when(step == (5, groups + 2, groups + 4, groups + 6)[k])
        def _(k=k):
            for j in range(1, inner):
                along_inner(k, j).wait_recv()
                to_core(k, j).start()

    @pl.when(step == groups)
    def _():
        pltpu.make_async_copy(own_ref, all_ref.at[block], local).wait()

    for k in range(outer):
        for j in range(inner):

            @pl.when(step == groups + j * 2 * outer + 2 * k + 1)
            def _(k=k, j=j):
                to_core(k, j).wait_recv()

    @pl.when(step == 2 * groups - 1)
    def _():
        for k in range(1, outer):
            along_outer(k).wait_send()
        for k in range(outer):
            for j in range(1, inner):
                along_inner(k, j).wait_send()
            for j in range(inner):
                to_core(k, j).wait_send()

    turn = jnp.maximum(step - groups, 0)
    z = lax.rem(block // (2 * inner) + outer - lax.rem(turn // 2, outer), outer)
    x = lax.rem(lax.rem(block // 2, inner) + inner - turn // (2 * outer), inner)
    core = lax.rem(lax.rem(block, 2) + turn, 2)
    return (z * inner + x) * 2 + core


def order_rows(groups, cap, owner, dest_ref, code_ref, x_ref, m_ref, proj_ref, rows_ref, slots_ref, rank_ref):
    count = dest_ref.shape[1]

    @pl.when(owner == 0)
    def _():
        width = 256
        before = lax.broadcasted_iota(jnp.int32, (width, width), 0)
        after = lax.broadcasted_iota(jnp.int32, (width, width), 1)
        upper = jnp.where(before <= after, 1.0, 0.0).astype(BF16)
        carry = jnp.zeros((groups, 1), F32)
        slots = jnp.zeros((groups, cap), F32)
        for at in range(0, count, width):
            span = pl.ds(at, width)
            owners = lax.broadcasted_iota(jnp.int32, (groups, width), 0)
            onehot = jnp.where(owners == dest_ref[:, span], 1.0, 0.0)
            running = plain(onehot.astype(BF16), upper) + carry
            rank = (jnp.sum(running * onehot, axis=0, keepdims=True) - 1.0).astype(jnp.int32)
            rank_ref[:, span] = rank
            carry = running[:, width - 1 : width]
            places = lax.broadcasted_iota(jnp.int32, (cap, width), 0)
            placed = jnp.where(places == rank, 1.0, 0.0).astype(BF16)
            slots = slots + over_columns((onehot * code_ref[:, span]).astype(BF16), placed)
        slots_ref[...] = slots

    rows = jnp.zeros((cap, x_ref.shape[1]), F32)
    places = lax.broadcasted_iota(jnp.int32, (cap, LANES), 0)
    for at in range(0, count, LANES):
        span = pl.ds(at, LANES)
        mine = jnp.where(dest_ref[:, span] == owner, rank_ref[:, span], -1)
        placed = jnp.where(places == mine, 1.0, 0.0).astype(BF16)
        rows = rows + plain(placed, x_ref[span, :])
    rows = rows.astype(BF16)
    rows_ref[owner] = rows
    proj_ref[owner] = plain(rows, m_ref[...]).astype(BF16)


def score_block(
    groups, cap, grad_scale, turn, owner,
    dest_ref, rank_ref, slots_ref, m_ref, proj_ref, rows_ref, census_ref,
    link_ref, sym_ref, total_ref, sums_ref,
):
    count = dest_ref.shape[1]
    feat = rows_ref.shape[2]
    hidden = m_ref.shape[1]
    people = census_ref.shape[1] - 16

    census = census_ref[owner, :people, :]
    labels = census_ref[owner, people:, :].astype(F32)
    columns = []
    for part in range(people // feat):
        row = jnp.broadcast_to(labels[part : part + 1, :], (128, feat))
        columns.append(jnp.transpose(row)[:, :1])
    label = jnp.concatenate(columns, axis=0)
    key = jnp.floor((label - 1.0) * 0.25)
    slot_label = slots_ref[pl.ds(owner, 1), :]
    slot_key = jnp.floor((slot_label - 1.0) * 0.25)

    mapped = plain(census, m_ref[...]).astype(BF16)
    raw = over_columns(mapped, proj_ref[owner])
    prob = 0.5 * jnp.tanh(raw * (0.5 / hidden**0.5)) + 0.5
    prob = jnp.where(key == slot_key, prob, 0.0)
    sums_ref[pl.ds(owner, 1), :] = jnp.sum(prob, axis=0, keepdims=True)
    resid = (prob - jnp.where(label == slot_label, 1.0, 0.0)).astype(BF16)
    pulled = plain(resid, rows_ref[owner])
    high = pulled.astype(BF16)
    low = (pulled - high.astype(F32)).astype(BF16)
    step = over_rows(census, high) + over_rows(census, low)

    @pl.when(turn == 0)
    def _():
        total_ref[...] = step

    @pl.when(turn > 0)
    def _():
        total_ref[...] += step

    @pl.when(turn == groups - 1)
    def _():
        total = total_ref[...]
        sym_ref[...] = (total + jnp.transpose(total)) * grad_scale
        sums = sums_ref[...]
        top = sums.astype(BF16)
        rest = (sums - top.astype(F32)).astype(BF16)
        places = lax.broadcasted_iota(jnp.int32, (cap, LANES), 0)
        owners = lax.broadcasted_iota(jnp.int32, (groups, LANES), 0)
        for at in range(0, count, LANES):
            span = pl.ds(at, LANES)
            onehot = jnp.where(owners == dest_ref[:, span], 1.0, 0.0).astype(BF16)
            spread = over_rows(top, onehot) + over_rows(rest, onehot)
            spread = jnp.where(places == rank_ref[:, span], spread, 0.0)
            link_ref[:, span] = jnp.sum(spread, axis=0, keepdims=True)


def link_kernel(
    groups, cap, grad_scale, dest_ref, code_ref, x_ref, m_ref, own_ref, link_ref, sym_ref,
    proj_ref, rows_ref, slots_ref, rank_ref, all_ref, total_ref, sums_ref, local, *sems,
):
    step = pl.program_id(0)
    owner = gather_step(groups, step, own_ref, all_ref, local, *sems)

    @pl.when(step < groups)
    def _():
        order_rows(
            groups, cap, step, dest_ref, code_ref, x_ref, m_ref, proj_ref, rows_ref, slots_ref, rank_ref
        )

    @pl.when(step >= groups)
    def _():
        score_block(
            groups, cap, grad_scale, step - groups, owner,
            dest_ref, rank_ref, slots_ref, m_ref, proj_ref, rows_ref, all_ref,
            link_ref, sym_ref, total_ref, sums_ref,
        )


def reduce_kernel(groups, regions, sym_ref, m_ref, grad_ref, got, mid, send1, recv1, send2, recv2):
    block = lax.axis_index("block")
    region = lax.axis_index("geo")
    rows = got.shape[1]
    cols = grad_ref.shape[1]
    barrier = pltpu.get_barrier_semaphore()
    for k in range(1, groups):
        pl.semaphore_signal(
            barrier, inc=1, device_id={"block": lax.rem(block + k, groups)}, device_id_type=MESH
        )
    for k in range(1, regions):
        pl.semaphore_signal(
            barrier, inc=1, device_id={"geo": lax.rem(region + k, regions)}, device_id_type=MESH
        )
    pl.semaphore_wait(barrier, groups + regions - 2)

    copies = []
    for k in range(1, groups):
        peer = lax.rem(block + k, groups)
        copy = pltpu.make_async_remote_copy(
            src_ref=sym_ref.at[pl.ds(pl.multiple_of(peer * rows, rows), rows), :],
            dst_ref=got.at[k],
            send_sem=send1.at[k],
            recv_sem=recv1.at[k],
            device_id={"block": peer},
            device_id_type=MESH,
        )
        copy.start()
        copies.append(copy)
    total = sym_ref[pl.ds(pl.multiple_of(block * rows, rows), rows), :]
    for k in range(1, groups):
        copies[k - 1].wait_recv()
        total = total + got[k]
    mid[0] = total
    crossing = []
    for k in range(1, regions):
        copy = pltpu.make_async_remote_copy(
            src_ref=mid.at[0],
            dst_ref=mid.at[k],
            send_sem=send2.at[k],
            recv_sem=recv2.at[k],
            device_id={"geo": lax.rem(region + k, regions)},
            device_id_type=MESH,
        )
        copy.start()
        crossing.append(copy)
    for k in range(1, regions):
        crossing[k - 1].wait_recv()
        total = total + mid[k]
    model = m_ref[:, pl.ds(pl.multiple_of(region * cols, cols), cols)]
    first = total.astype(BF16)
    left = total - first.astype(F32)
    second = left.astype(BF16)
    third = (left - second.astype(F32)).astype(BF16)
    grad_ref[...] = plain(first, model) + plain(second, model) + plain(third, model)
    for copy in copies + crossing:
        copy.wait_send()


def body(
    admin_vectors,
    admin_bucket,
    admin_person_class,
    admin_holder_bucket,
    population_vectors,
    population_bucket,
    population_person_class,
    model_coefficients,
):
    count, feat = admin_vectors.shape
    groups = lax.axis_size("block")
    regions = lax.axis_size("geo")
    cap = 3 * count // (2 * groups)
    hidden = model_coefficients.shape[1]
    people = population_vectors.shape[0]
    dest = admin_holder_bucket.reshape(1, count)
    code = (admin_bucket * 4 + admin_person_class + 1).astype(F32).reshape(1, count)
    census_code = (population_bucket * 4 + population_person_class + 1).astype(BF16)
    census_code = census_code.reshape(people // feat, feat)
    census_code = jnp.pad(census_code, ((0, 16 - people // feat), (0, 0)))
    census = jnp.concatenate([population_vectors, census_code], axis=0)
    tall = people + 16

    def whole(shape):
        return pl.BlockSpec(shape, lambda o: (0,) * len(shape))

    grad_scale = 1.0 / hidden**0.5 / (count * groups * regions) ** 0.5
    link, sym = pl.pallas_call(
        functools.partial(link_kernel, groups, cap, grad_scale),
        grid=(2 * groups,),
        in_specs=[whole((1, count)), whole((1, count)), whole((count, feat)), whole((feat, hidden))]
        + [pl.BlockSpec(memory_space=pl.ANY)],
        out_specs=[whole((1, count)), whole((feat, feat))],
        out_shape=[jax.ShapeDtypeStruct((1, count), F32), jax.ShapeDtypeStruct((feat, feat), F32)],
        scratch_shapes=[
            pltpu.VMEM((groups, cap, hidden), BF16),
            pltpu.VMEM((groups, cap, feat), BF16),
            pltpu.VMEM((groups, cap), F32),
            pltpu.VMEM((1, count), jnp.int32),
            pltpu.VMEM((groups, tall, feat), BF16),
            pltpu.VMEM((feat, feat), F32),
            pltpu.VMEM((groups, cap), F32),
            pltpu.SemaphoreType.DMA,
        ]
        + [pltpu.SemaphoreType.DMA((4,))] * 2
        + [pltpu.SemaphoreType.DMA((groups // 2,))] * 4,
        compiler_params=pltpu.CompilerParams(
            vmem_limit_bytes=48 << 20, collective_id=1, has_side_effects=True
        ),
        cost_estimate=pl.CostEstimate(
            flops=2 * groups * cap * feat * (count + hidden)
            + 2 * groups * people * (feat * hidden + cap * hidden + cap * feat + 2 * feat * feat),
            bytes_accessed=10 << 20,
            transcendentals=groups * people * cap,
        ),
        name="link_records",
    )(dest, code, admin_vectors, model_coefficients, census)

    rows_each = feat // groups
    cols_each = hidden // regions
    grad = pl.pallas_call(
        functools.partial(reduce_kernel, groups, regions),
        in_specs=[pl.BlockSpec(memory_space=pltpu.VMEM)] * 2,
        out_specs=pl.BlockSpec(memory_space=pltpu.VMEM),
        out_shape=jax.ShapeDtypeStruct((rows_each, cols_each), F32),
        scratch_shapes=[
            pltpu.VMEM((groups, rows_each, feat), F32),
            pltpu.VMEM((regions, rows_each, feat), F32),
            pltpu.SemaphoreType.DMA((groups,)),
            pltpu.SemaphoreType.DMA((groups,)),
            pltpu.SemaphoreType.DMA((regions,)),
            pltpu.SemaphoreType.DMA((regions,)),
        ],
        compiler_params=pltpu.CompilerParams(collective_id=0, has_side_effects=True),
        cost_estimate=pl.CostEstimate(
            flops=6 * rows_each * cols_each * feat, bytes_accessed=1 << 20, transcendentals=0
        ),
        name="reduce_gradient",
    )(sym, model_coefficients)
    return (link.reshape(count), grad)


def solution(mesh):
    placed = (
        P(("block", "geo"), None),
        P(("block", "geo")),
        P(("block", "geo")),
        P(("block", "geo"), None),
        P(("block", "geo"), None),
        P(("block", "geo")),
        P(("block", "geo")),
        P(),
    )
    return jax.shard_map(
        body,
        mesh=mesh,
        in_specs=placed,
        out_specs=(P(("block", "geo")), P("block", "geo")),
        check_vma=False,
    )
```
